32 devices in a mesh: dp: 4 (over y, x), tensor: 8 (over z, core).
Axes of the slice: x: 2, y: 2, z: 4, core: 2. Of those that a mesh axis runs over, the one named last changes fastest.
Arguments:
- tokens: bfloat16 [128, 8192], P(('dp', 'tensor')), may hold values from -16 to 16
- gate_weight: bfloat16 [8192, 16384], P('dp', 'tensor'), may hold values from -0.0625 to 0.0625
- up_weight: bfloat16 [8192, 16384], P('dp', 'tensor'), may hold values from -0.0625 to 0.0625
- cotangent: bfloat16 [128, 16384], P('dp', 'tensor'), may hold values from -13 to 13
Outputs:
- hidden: bfloat16 [128, 16384], P('dp', 'tensor')
- grad_tokens: bfloat16 [128, 8192], P(('dp', 'tensor'))
- grad_gate: bfloat16 [8192, 16384], P('dp', 'tensor')
- grad_up: bfloat16 [8192, 16384], P('dp', 'tensor')
- token_descale: float32 [], replicated
- grad_descale: float32 [], replicated
The draws below stay inside these ranges and needn't reach their ends.
All inputs are finite; a program needn't handle non-finite values. Where the reference program divides by a largest or mean magnitude, that divisor is 1e-20 or more.
Results may differ from the reference program's by a relative error of at most 0.02.
Values may be sent and summed in bfloat16 or wider, within the bound.
A program may use at most 256 MiB of HBM per device.

```python
import jax
import jax.numpy as jnp
from jax import lax

D = 8192
FF = 16384
TOK_REP = 32
TOKENS = 128
N_DP = 4
N_TENSOR = 8


def draw_tokens(key, part):
    key = jax.random.fold_in(key, 11)
    base_key, row_key = jax.random.split(key)
    position = jnp.arange(TOKENS, dtype=jnp.float32) / TOKENS
    jitter = jax.random.uniform(row_key, (TOKENS,), jnp.float32)
    base = jax.random.truncated_normal(base_key, -4.0, 4.0, (TOKENS, D), jnp.float32)
    row_scale = 10.0 ** (0.6 * position + 0.4 * jitter)
    value_entries = base * row_scale[:, None] * 0.3
    return value_entries.astype(jnp.bfloat16)


def draw_cotangent(key, part):
    key = jax.random.fold_in(key, 23)
    base_key, col_key = jax.random.split(key)
    position = jnp.arange(FF, dtype=jnp.float32) / FF
    jitter = jax.random.uniform(col_key, (FF,), jnp.float32)
    base = jax.random.truncated_normal(base_key, -4.0, 4.0, (TOKENS, FF), jnp.float32)
    col_scale = 10.0 ** (0.8 * position + 0.3 * jitter)
    value_entries = base * col_scale[None, :] * 0.25
    return value_entries.astype(jnp.bfloat16)


def shard_levels(stream_key, dims, cuts, least, largest):
    def one(axis_at, parts):
        steps = jax.random.uniform(jax.random.fold_in(jax.random.fold_in(stream_key, 6), axis_at), (parts,), jnp.float32, least / len(cuts), largest / len(cuts))
        return jnp.repeat(jnp.exp(steps), dims[axis_at] // parts).reshape((-1,) + (1,) * (len(dims) - axis_at - 1))

    gain = one(*cuts[0])
    for cut in cuts[1:]:
        gain = gain * one(*cut)
    return gain


def centred(rng, extent, spread, most, pieces=(), held_as=jnp.bfloat16):
    values = spread * jax.random.normal(rng, extent, jnp.float32)
    if pieces:
        values = values * shard_levels(rng, extent, pieces, -0.22, 0.18)
    return jnp.clip(values, -most, most).astype(held_as)


def setup_inputs(seed: int = 0) -> dict:
    keys = jax.random.split(jax.random.key(seed), 5)
    return {
        "tokens": draw_tokens(jax.random.fold_in(keys[4], 71), 0),
        "gate_weight": centred(keys[1], (D, FF), D ** -0.5, 0.0625, ((0, 4), (1, 8))),
        "up_weight": centred(keys[2], (D, FF), D ** -0.5, 0.0625, ((0, 4), (1, 8))),
        "cotangent": draw_cotangent(jax.random.fold_in(keys[4], 71), 0),
    }


FP_MAX = 448.0
EPSILON = 1e-6


def settle(value_entries):
    return lax.optimization_barrier(value_entries.astype(jnp.bfloat16)).astype(jnp.float32)


def reference(tokens, gate_weight, up_weight, cotangent):
    token_peak = jnp.max(jnp.abs(tokens)).astype(jnp.float32)
    token_descale = (token_peak + EPSILON) / FP_MAX
    quantized = (tokens.astype(jnp.float32) * (FP_MAX / (token_peak + EPSILON))).astype(jnp.bfloat16)
    slice_width = D // N_DP

    def add_slice(block, summed_totals):
        start = jnp.asarray(block, jnp.int32) * slice_width
        columns = lax.dynamic_slice_in_dim(quantized, start, slice_width, 1)
        gate_rows = lax.dynamic_slice_in_dim(gate_weight, start, slice_width, 0)
        up_rows = lax.dynamic_slice_in_dim(up_weight, start, slice_width, 0)
        gate_part = settle(jnp.dot(columns, gate_rows, preferred_element_type=jnp.float32))
        up_part = settle(jnp.dot(columns, up_rows, preferred_element_type=jnp.float32))
        return (summed_totals[0] + gate_part, summed_totals[1] + up_part)

    empty = jnp.zeros((TOKENS, FF), jnp.float32)
    gate_sum, up_sum = lax.fori_loop(0, N_DP, add_slice, (empty, empty))
    gate_act = gate_sum * token_descale
    up_act = up_sum * token_descale
    sigmoid_gate = jax.nn.sigmoid(gate_act)
    silu_gate = gate_act * sigmoid_gate
    hidden = (silu_gate * up_act).astype(jnp.bfloat16)
    cot_values = cotangent.astype(jnp.float32)
    gate_gradient = cot_values * up_act * sigmoid_gate * (1.0 + gate_act * (1.0 - sigmoid_gate))
    d_up = cot_values * silu_gate
    grad_peak = jnp.maximum(jnp.max(jnp.abs(gate_gradient)), jnp.max(jnp.abs(d_up)))
    grad_descale = (grad_peak + EPSILON) / FP_MAX
    grad_scale = FP_MAX / (grad_peak + EPSILON)
    gate_quant = (gate_gradient * grad_scale).astype(jnp.bfloat16)
    up_quant = (d_up * grad_scale).astype(jnp.bfloat16)
    shard_width = FF // N_TENSOR

    def add_shard(shard, total):
        start = jnp.asarray(shard, jnp.int32) * shard_width
        gate_cols = lax.dynamic_slice_in_dim(gate_quant, start, shard_width, 1)
        up_cols = lax.dynamic_slice_in_dim(up_quant, start, shard_width, 1)
        gate_block = lax.dynamic_slice_in_dim(gate_weight, start, shard_width, 1)
        up_block = lax.dynamic_slice_in_dim(up_weight, start, shard_width, 1)
        term = jnp.dot(gate_cols, gate_block.T, preferred_element_type=jnp.float32)
        term = term + jnp.dot(up_cols, up_block.T, preferred_element_type=jnp.float32)
        return total + settle(term * grad_descale)

    grad_tokens = lax.fori_loop(0, N_TENSOR, add_shard, jnp.zeros((TOKENS, D), jnp.float32)).astype(jnp.bfloat16)
    both_descale = token_descale * grad_descale
    contract = (((0,), (0,)), ((), ()))

    def add_replica(replica, summed_totals):
        start = jnp.asarray(replica, jnp.int32) * TOK_REP
        token_rows = lax.dynamic_slice_in_dim(quantized, start, TOK_REP, 0)
        gate_rows = lax.dynamic_slice_in_dim(gate_quant, start, TOK_REP, 0)
        up_rows = lax.dynamic_slice_in_dim(up_quant, start, TOK_REP, 0)
        gate_term = lax.dot_general(token_rows, gate_rows, contract, preferred_element_type=jnp.float32)
        up_term = lax.dot_general(token_rows, up_rows, contract, preferred_element_type=jnp.float32)
        return (summed_totals[0] + settle(gate_term * both_descale), summed_totals[1] + settle(up_term * both_descale))

    blank = jnp.zeros((D, FF), jnp.float32)
    grad_gate, grad_up = lax.fori_loop(0, N_DP, add_replica, (blank, blank))
    return (hidden, grad_tokens, grad_gate.astype(jnp.bfloat16), grad_up.astype(jnp.bfloat16), token_descale, grad_descale)
```

```python
import functools

import jax
import jax.numpy as jnp
import numpy as np
from jax import lax
from jax.experimental import pallas as pl
from jax.experimental.pallas import tpu as pltpu
from jax.sharding import PartitionSpec as P

FP_MAX = 448.0
EPSILON = 1e-06
CHUNKS = 4
MESH = pl.DeviceIdType.MESH
F32 = jnp.float32
BF16 = jnp.bfloat16


def remote(src, dst, send, recv, device):
    return pltpu.make_async_remote_copy(
        src_ref=src, dst_ref=dst, send_sem=send, recv_sem=recv, device_id=device, device_id_type=MESH
    )


def lane_peak(values, rows):
    peak = None
    for at in range(0, values.shape[0], rows):
        for lane in range(0, values.shape[1], 128):
            piece = values[at : at + rows, lane : lane + 128]
            peak = piece if peak is None else jnp.maximum(peak, piece)
    return peak


def exchange(
    nd, nt,
    tok, gate_hbm, up_hbm, cot, perm,
    hid, x, g, gtok, peaks,
    wg, wu, blocks, wide, xt, part, inbox, dx, dxp, pair_in, line_out, line_in, back,
    stats, st_dp, st_pair, st_line,
    w_sem, a_s, a_r, b_s, b_r, f_s, f_r, p_s, p_r, rs_s, rs_r, ag_s, ag_r,
    l_s, l_r, o_s, o_r, sd_s, sd_r, sp_s, sp_r, sl_s, sl_r,
):
    d = lax.axis_index("dp")
    t = lax.axis_index("tensor")
    core = lax.rem(t, 2)
    z = t // 2
    nz = nt // 2
    sib = t + 1 - 2 * core
    tl = tok.shape[0]
    s, units = gate_hbm.shape
    r = cot.shape[0]
    total = nd * r
    rows = nd * tl
    uc = units // CHUNKS
    tile = min(256, s)
    dp_to = [lax.rem(d + k, nd) for k in range(nd)]
    z_to = [lax.rem(z + k, nz) for k in range(nz)]
    z_from = [lax.rem(z + nz - k, nz) for k in range(nz)]

    def weight_copies(c):
        cols = pl.ds(pl.multiple_of(c * uc, 128), uc)
        return (
            pltpu.make_async_copy(gate_hbm.at[:, cols], wg.at[:, cols], w_sem.at[0, c]),
            pltpu.make_async_copy(up_hbm.at[:, cols], wu.at[:, cols], w_sem.at[1, c]),
        )

    for c in range(CHUNKS):
        for copy in weight_copies(c):
            copy.start()

    barrier = pltpu.get_barrier_semaphore()
    for k in range(1, nd):
        pl.semaphore_signal(barrier, inc=1, device_id=(dp_to[k], t), device_id_type=MESH)
    for k in range(1, nz):
        pl.semaphore_signal(barrier, inc=1, device_id=(d, 2 * z_to[k] + core), device_id_type=MESH)
    pl.semaphore_signal(barrier, inc=1, device_id=(d, sib), device_id_type=MESH)
    pl.semaphore_wait(barrier, nd + nz - 1)

    def feature_cols(i):
        return pl.ds(pl.multiple_of(i * s, 128), s)

    sends = []
    first = []
    for k in range(1, nd):
        copy = remote(tok.at[:, feature_cols(dp_to[k])], blocks.at[d], a_s.at[k], a_r.at[k], (dp_to[k], t))
        copy.start()
        first.append(copy)
    blocks[d] = tok[:, feature_cols(d)]
    token_peak = lane_peak(jnp.abs(tok[...].astype(F32)), tl)
    stats[0] = jnp.broadcast_to(jnp.max(token_peak, axis=0, keepdims=True), (8, 128))
    for copy in first:
        copy.wait_recv()
    sends += first
    for i in range(nd):
        wide[i * tl : (i + 1) * tl, :] = blocks[i].astype(F32)
    xt[t] = wide[...].astype(BF16)

    along = [
        remote(xt.at[t], xt.at[t], b_s.at[k], b_r.at[k], (d, 2 * z_to[k] + core)) for k in range(1, nz)
    ]
    for copy in along:
        copy.start()
    across = [remote(xt.at[t], xt.at[t], f_s.at[0], f_r.at[0], (d, sib))]
    across[0].start()
    for k in range(1, nz):
        along[k - 1].wait_recv()
        slot = 2 * z_from[k] + core
        copy = remote(xt.at[slot], xt.at[slot], f_s.at[k], f_r.at[k], (d, sib))
        copy.start()
        across.append(copy)
    for copy in across:
        copy.wait_recv()
    sends += along + across

    @pl.loop(0, s // tile)
    def _(j):
        cols = pl.ds(pl.multiple_of(j * tile, 128), tile)
        lined = xt[:, :, cols].reshape(total, tile)
        x[:, cols] = jnp.dot(perm[0], lined, preferred_element_type=F32).astype(BF16)
        dx[:, cols] = jnp.zeros((total, tile), F32)

    def partial_copy(c, k):
        return remote(part.at[c, dp_to[k]], inbox.at[c, k - 1], rs_s.at[c, k], rs_r.at[c, k], (dp_to[k], t))

    wide_tile = min(256, uc)

    @pl.loop(0, CHUNKS)
    def _(c):
        for copy in weight_copies(c):
            copy.wait()
        for side, w in ((0, wg), (1, wu)):
            for at in range(0, uc, wide_tile):
                cols = pl.ds(pl.multiple_of(c * uc + at, 128), wide_tile)
                product = jnp.dot(x[...], w[:, cols], preferred_element_type=F32)
                part[c, :, side, :, at : at + wide_tile] = product.astype(BF16).reshape(nd, r, wide_tile)
        for k in range(1, nd):
            partial_copy(c, k).start()

    def grad_copy(c, k):
        return remote(g.at[c, d], g.at[c, d], ag_s.at[c, k], ag_r.at[c, k], (dp_to[k], t))

    def activate(c, peak):
        for k in range(1, nd):
            partial_copy(c, k).wait_recv()
        cols = pl.ds(pl.multiple_of(c * uc, 128), uc)
        gate = part[c, d, 0].astype(F32)
        up = part[c, d, 1].astype(F32)
        for k in range(1, nd):
            gate = gate + inbox[c, k - 1, 0].astype(F32)
            up = up + inbox[c, k - 1, 1].astype(F32)
        sig = jax.nn.sigmoid(gate)
        silu = gate * sig
        hid[:, cols] = (silu * up).astype(BF16)
        cotangent = cot[:, cols].astype(F32)
        d_gate = cotangent * up * sig * (1.0 + gate * (1.0 - sig))
        d_up = cotangent * silu
        g[c, d, 0] = d_gate.astype(BF16)
        g[c, d, 1] = d_up.astype(BF16)
        for k in range(1, nd):
            grad_copy(c, k).start()
        return jnp.maximum(peak, lane_peak(jnp.maximum(jnp.abs(d_gate), jnp.abs(d_up)), 8))

    stats[1] = lax.fori_loop(0, CHUNKS, activate, jnp.zeros((8, 128), F32))
    peak_dp = [remote(stats, st_dp.at[k - 1], sd_s.at[k], sd_r.at[k], (dp_to[k], t)) for k in range(1, nd)]
    for copy in peak_dp:
        copy.start()

    contract = (((1,), (1,)), ((), ()))

    @pl.loop(0, CHUNKS)
    def _(c):
        for k in range(1, nd):
            grad_copy(c, k).wait_recv()
        units_here = pl.ds(pl.multiple_of(c * uc, 128), uc)

        @pl.loop(0, s // tile)
        def _(j):
            cols = pl.ds(pl.multiple_of(j * tile, 128), tile)
            one = lax.dot_general(
                g[c, :, 0].reshape(total, uc), wg[cols, units_here], contract, preferred_element_type=F32
            )
            two = lax.dot_general(
                g[c, :, 1].reshape(total, uc), wu[cols, units_here], contract, preferred_element_type=F32
            )
            dx[:, cols] += one + two

    @pl.loop(0, s // tile)
    def _(j):
        cols = pl.ds(pl.multiple_of(j * tile, 128), tile)
        lined = jnp.dot(perm[1], dx[:, cols].astype(BF16), preferred_element_type=F32)
        dxp[:, :, :, cols] = lined.astype(BF16).reshape(2, nz, rows, tile)

    pair = remote(dxp.at[1 - core], pair_in, p_s, p_r, (d, sib))
    pair.start()
    for copy in peak_dp:
        copy.wait()
    peak = stats[...]
    for k in range(1, nd):
        peak = jnp.maximum(peak, st_dp[k - 1])
    stats[...] = peak
    peak_pair = remote(stats, st_pair, sp_s, sp_r, (d, sib))
    peak_pair.start()
    pair.wait_recv()
    line = []
    for k in range(1, nz):
        mixed = dxp[core, z_to[k]].astype(F32) + pair_in[z_to[k]].astype(F32)
        line_out[k - 1] = mixed.astype(BF16)
        copy = remote(line_out.at[k - 1], line_in.at[k - 1], l_s.at[k], l_r.at[k], (d, 2 * z_to[k] + core))
        copy.start()
        line.append(copy)
    peak_pair.wait()
    stats[...] = jnp.maximum(stats[...], st_pair[...])
    peak_line = [
        remote(stats, st_line.at[k - 1], sl_s.at[k], sl_r.at[k], (d, 2 * z_to[k] + core))
        for k in range(1, nz)
    ]
    for copy in peak_line:
        copy.start()
    reduced = dxp[core, z].astype(F32) + pair_in[z].astype(F32)
    for copy in line:
        copy.wait_recv()
    for k in range(1, nz):
        reduced = reduced + line_in[k - 1].astype(F32)
    wide[...] = reduced
    for i in range(nd):
        back[i] = wide[i * tl : (i + 1) * tl, :].astype(BF16)
    home = [
        remote(back.at[dp_to[k]], gtok.at[:, feature_cols(d)], o_s.at[k], o_r.at[k], (dp_to[k], t))
        for k in range(1, nd)
    ]
    for copy in home:
        copy.start()
    gtok[:, feature_cols(d)] = back[d]
    for copy in peak_line:
        copy.wait()
    peak = stats[...]
    for k in range(1, nz):
        peak = jnp.maximum(peak, st_line[k - 1])
    peaks[...] = peak
    for copy in sends + line + [pair]:
        copy.wait_send()

    @pl.loop(0, CHUNKS)
    def _(c):
        for k in range(1, nd):
            partial_copy(c, k).wait_send()
            grad_copy(c, k).wait_send()

    for copy in home:
        copy.wait()


def weight_grads(x, g, gate_out, up_out):
    chunks, nd, _, r, uc = g.shape
    contract = (((0,), (0,)), ((), ()))
    for side, out in ((0, gate_out), (1, up_out)):
        for c in range(chunks):
            out[:, c * uc : (c + 1) * uc] = lax.dot_general(
                x[...], g[c, :, side].reshape(nd * r, uc), contract, preferred_element_type=F32
            ).astype(BF16)


def orders(nd, nt, tl):
    total = nd * nt * tl
    index = np.arange(total).reshape(nd, nt, tl)
    arrived = np.arange(total).reshape(nt, nd, tl).transpose(1, 0, 2).reshape(-1)
    leaving = index.reshape(nd, nt // 2, 2, tl).transpose(2, 1, 0, 3).reshape(-1)
    eye = np.eye(total, dtype=np.float32)
    return jnp.asarray(np.stack([eye[arrived], eye[leaving]]), BF16)


def local(nd, nt, tokens, gate_weight, up_weight, cotangent):
    tl, _ = tokens.shape
    s, units = gate_weight.shape
    r = cotangent.shape[0]
    total = nd * r
    rows = nd * tl
    nz = nt // 2
    uc = units // CHUNKS
    dma = pltpu.SemaphoreType.DMA
    vmem = pl.BlockSpec(memory_space=pltpu.VMEM)
    hbm = pl.BlockSpec(memory_space=pl.ANY)
    weight_bytes = 2 * s * units * 2
    hidden, x, g, grad_tokens, peaks = pl.pallas_call(
        functools.partial(exchange, nd, nt),
        out_shape=(
            jax.ShapeDtypeStruct((r, units), BF16),
            jax.ShapeDtypeStruct((total, s), BF16),
            jax.ShapeDtypeStruct((CHUNKS, nd, 2, r, uc), BF16),
            jax.ShapeDtypeStruct((tl, nd * s), BF16),
            jax.ShapeDtypeStruct((2, 8, 128), F32),
        ),
        in_specs=[vmem, hbm, hbm, vmem, vmem],
        out_specs=(vmem,) * 5,
        scratch_shapes=[
            pltpu.VMEM((s, units), BF16),
            pltpu.VMEM((s, units), BF16),
            pltpu.VMEM((nd, tl, s), BF16),
            pltpu.VMEM((rows, s), F32),
            pltpu.VMEM((nt, rows, s), BF16),
            pltpu.VMEM((CHUNKS, nd, 2, r, uc), BF16),
            pltpu.VMEM((CHUNKS, nd - 1, 2, r, uc), BF16),
            pltpu.VMEM((total, s), F32),
            pltpu.VMEM((2, nz, rows, s), BF16),
            pltpu.VMEM((nz, rows, s), BF16),
            pltpu.VMEM((nz - 1, rows, s), BF16),
            pltpu.VMEM((nz - 1, rows, s), BF16),
            pltpu.VMEM((nd, tl, s), BF16),
            pltpu.VMEM((2, 8, 128), F32),
            pltpu.VMEM((nd - 1, 2, 8, 128), F32),
            pltpu.VMEM((2, 8, 128), F32),
            pltpu.VMEM((nz - 1, 2, 8, 128), F32),
            dma((2, CHUNKS)),
            dma((nd,)), dma((nd,)),
            dma((nz,)), dma((nz,)),
            dma((nz,)), dma((nz,)),
            dma, dma,
            dma((CHUNKS, nd)), dma((CHUNKS, nd)),
            dma((CHUNKS, nd)), dma((CHUNKS, nd)),
            dma((nz,)), dma((nz,)),
            dma((nd,)), dma((nd,)),
            dma((nd,)), dma((nd,)),
            dma, dma,
            dma((nz,)), dma((nz,)),
        ],
        compiler_params=pltpu.CompilerParams(
            collective_id=0, has_side_effects=True, vmem_limit_bytes=48 * 2**20
        ),
        cost_estimate=pl.CostEstimate(
            flops=8 * total * s * units, bytes_accessed=weight_bytes, transcendentals=r * units
        ),
    )(tokens, gate_weight, up_weight, cotangent, orders(nd, nt, tl))

    tile = min(256, s)
    grad_gate, grad_up = pl.pallas_call(
        weight_grads,
        grid=(s // tile,),
        out_shape=(jax.ShapeDtypeStruct((s, units), BF16),) * 2,
        in_specs=[
            pl.BlockSpec((total, tile), lambda i: (0, i)),
            pl.BlockSpec((CHUNKS, nd, 2, r, uc), lambda i: (0, 0, 0, 0, 0)),
        ],
        out_specs=(pl.BlockSpec((tile, units), lambda i: (i, 0)),) * 2,
        compiler_params=pltpu.CompilerParams(vmem_limit_bytes=32 * 2**20),
        cost_estimate=pl.CostEstimate(
            flops=4 * total * s * units, bytes_accessed=weight_bytes, transcendentals=0
        ),
    )(x, g)
    descales = (jnp.max(peaks, axis=(1, 2)) + EPSILON) / FP_MAX
    return (hidden, grad_tokens, grad_gate, grad_up, descales[0], descales[1])


def solution(mesh):
    nd = mesh.shape["dp"]
    nt = mesh.shape["tensor"]
    return jax.shard_map(
        functools.partial(local, nd, nt),
        mesh=mesh,
        in_specs=(
            P(("dp", "tensor"), None),
            P("dp", "tensor"),
            P("dp", "tensor"),
            P("dp", "tensor"),
        ),
        out_specs=(
            P("dp", "tensor"),
            P(("dp", "tensor"), None),
            P("dp", "tensor"),
            P("dp", "tensor"),
            P(),
            P(),
        ),
        check_vma=False,
    )
```

```python
import functools

import jax
import jax.numpy as jnp
from jax import lax
from jax.experimental import pallas as pl
from jax.experimental.pallas import tpu as pltpu
from jax.sharding import PartitionSpec as P

FP_MAX = 448.0
EPSILON = 1e-06
CHUNKS = 4
MESH = pl.DeviceIdType.MESH
F32 = jnp.float32
BF16 = jnp.bfloat16


def remote(src, dst, send, recv, device):
    return pltpu.make_async_remote_copy(
        src_ref=src, dst_ref=dst, send_sem=send, recv_sem=recv, device_id=device, device_id_type=MESH
    )


def lane_peak(values, rows):
    peak = None
    for at in range(0, values.shape[0], rows):
        for lane in range(0, values.shape[1], 128):
            piece = values[at : at + rows, lane : lane + 128]
            peak = piece if peak is None else jnp.maximum(peak, piece)
    return peak


def exchange(
    nd, nt,
    tok, gate_hbm, up_hbm, cot,
    hid, x, g, gtok, peaks,
    perm, wg, wu, blocks, wide, xt, part, inbox, dx, dxp, pair_in, line_out, line_in, back,
    stats, st_dp, st_pair, st_line,
    w_sem, a_s, a_r, b_s, b_r, f_s, f_r, p_s, p_r, rs_s, rs_r, ag_s, ag_r,
    l_s, l_r, o_s, o_r, sd_s, sd_r, sp_s, sp_r, sl_s, sl_r,
):
    d = lax.axis_index("dp")
    t = lax.axis_index("tensor")
    core = lax.rem(t, 2)
    z = t // 2
    nz = nt // 2
    sib = t + 1 - 2 * core
    tl = tok.shape[0]
    s, units = gate_hbm.shape
    r = cot.shape[0]
    total = nd * r
    rows = nd * tl
    uc = units // CHUNKS
    tile = min(256, s)
    dp_to = [lax.rem(d + k, nd) for k in range(nd)]
    z_to = [lax.rem(z + k, nz) for k in range(nz)]
    z_from = [lax.rem(z + nz - k, nz) for k in range(nz)]

    def weight_copies(c):
        cols = pl.ds(pl.multiple_of(c * uc, 128), uc)
        return (
            pltpu.make_async_copy(gate_hbm.at[:, cols], wg.at[:, cols], w_sem.at[0, c]),
            pltpu.make_async_copy(up_hbm.at[:, cols], wu.at[:, cols], w_sem.at[1, c]),
        )

    barrier = pltpu.get_barrier_semaphore()
    for k in range(1, nd):
        pl.semaphore_signal(barrier, inc=1, device_id=(dp_to[k], t), device_id_type=MESH)
    for k in range(1, nz):
        pl.semaphore_signal(barrier, inc=1, device_id=(d, 2 * z_to[k] + core), device_id_type=MESH)
    pl.semaphore_signal(barrier, inc=1, device_id=(d, sib), device_id_type=MESH)
    pl.semaphore_wait(barrier, nd + nz - 1)

    def feature_cols(i):
        return pl.ds(pl.multiple_of(i * s, 128), s)

    sends = []
    first = []
    for k in range(1, nd):
        copy = remote(tok.at[:, feature_cols(dp_to[k])], blocks.at[d], a_s.at[k], a_r.at[k], (dp_to[k], t))
        copy.start()
        first.append(copy)
    for c in range(CHUNKS):
        for copy in weight_copies(c):
            copy.start()

    blocks[d] = tok[:, feature_cols(d)]
    token_peak = lane_peak(jnp.abs(tok[...].astype(F32)), tl)
    stats[0] = jnp.broadcast_to(jnp.max(token_peak, axis=0, keepdims=True), (8, 128))
    for copy in first:
        copy.wait_recv()
    sends += first
    for i in range(nd):
        wide[i * tl : (i + 1) * tl, :] = blocks[i].astype(F32)
    xt[t] = wide[...].astype(BF16)

    along = [
        remote(xt.at[t], xt.at[t], b_s.at[k], b_r.at[k], (d, 2 * z_to[k] + core)) for k in range(1, nz)
    ]
    for copy in along:
        copy.start()
    across = [remote(xt.at[t], xt.at[t], f_s.at[0], f_r.at[0], (d, sib))]
    across[0].start()
    row = lax.broadcasted_iota(jnp.int32, (total, 1), 0)
    col = lax.broadcasted_iota(jnp.int32, (total, total), 1)
    inner = lax.rem(row, tl)
    arrived = lax.rem(lax.div(row, tl), nt) * rows + lax.div(row, r) * tl + inner
    end = lax.div(row, rows)
    tensor_at = 2 * lax.rem(end, nz) + lax.div(end, nz)
    leaving = lax.rem(lax.div(row, tl), nd) * r + tensor_at * tl + inner
    for i, order in enumerate((arrived, leaving)):
        perm[i] = jnp.where(col == order, 1.0, 0.0).astype(BF16)
    for k in range(1, nz):
        along[k - 1].wait_recv()
        slot = 2 * z_from[k] + core
        copy = remote(xt.at[slot], xt.at[slot], f_s.at[k], f_r.at[k], (d, sib))
        copy.start()
        across.append(copy)
    for copy in across:
        copy.wait_recv()
    sends += along + across

    @pl.loop(0, s // tile)
    def _(j):
        cols = pl.ds(pl.multiple_of(j * tile, 128), tile)
        lined = xt[:, :, cols].reshape(total, tile)
        x[:, cols] = jnp.dot(perm[0], lined, preferred_element_type=F32).astype(BF16)
        dx[:, cols] = jnp.zeros((total, tile), F32)

    def partial_copy(c, k):
        return remote(part.at[c, dp_to[k]], inbox.at[c, k - 1], rs_s.at[c, k], rs_r.at[c, k], (dp_to[k], t))

    wide_tile = min(256, uc)

    @pl.loop(0, CHUNKS)
    def _(c):
        for copy in weight_copies(c):
            copy.wait()
        for side, w in ((0, wg), (1, wu)):
            for at in range(0, uc, wide_tile):
                cols = pl.ds(pl.multiple_of(c * uc + at, 128), wide_tile)
                product = jnp.dot(x[...], w[:, cols], preferred_element_type=F32)
                part[c, :, side, :, at : at + wide_tile] = product.astype(BF16).reshape(nd, r, wide_tile)
        for k in range(1, nd):
            partial_copy(c, k).start()

    def grad_copy(c, k):
        return remote(g.at[c, d], g.at[c, d], ag_s.at[c, k], ag_r.at[c, k], (dp_to[k], t))

    def activate(c, peak):
        for k in range(1, nd):
            partial_copy(c, k).wait_recv()
        cols = pl.ds(pl.multiple_of(c * uc, 128), uc)
        gate = part[c, d, 0].astype(F32)
        up = part[c, d, 1].astype(F32)
        for k in range(1, nd):
            gate = gate + inbox[c, k - 1, 0].astype(F32)
            up = up + inbox[c, k - 1, 1].astype(F32)
        sig = jax.nn.sigmoid(gate)
        silu = gate * sig
        hid[:, cols] = (silu * up).astype(BF16)
        cotangent = cot[:, cols].astype(F32)
        d_gate = cotangent * up * sig * (1.0 + gate * (1.0 - sig))
        d_up = cotangent * silu
        g[c, d, 0] = d_gate.astype(BF16)
        g[c, d, 1] = d_up.astype(BF16)
        for k in range(1, nd):
            grad_copy(c, k).start()
        return jnp.maximum(peak, lane_peak(jnp.maximum(jnp.abs(d_gate), jnp.abs(d_up)), 8))

    stats[1] = lax.fori_loop(0, CHUNKS, activate, jnp.zeros((8, 128), F32))
    peak_dp = [remote(stats, st_dp.at[k - 1], sd_s.at[k], sd_r.at[k], (dp_to[k], t)) for k in range(1, nd)]
    for copy in peak_dp:
        copy.start()

    contract = (((1,), (1,)), ((), ()))

    @pl.loop(0, CHUNKS)
    def _(c):
        for k in range(1, nd):
            grad_copy(c, k).wait_recv()
        units_here = pl.ds(pl.multiple_of(c * uc, 128), uc)

        @pl.loop(0, s // tile)
        def _(j):
            cols = pl.ds(pl.multiple_of(j * tile, 128), tile)
            one = lax.dot_general(
                g[c, :, 0].reshape(total, uc), wg[cols, units_here], contract, preferred_element_type=F32
            )
            two = lax.dot_general(
                g[c, :, 1].reshape(total, uc), wu[cols, units_here], contract, preferred_element_type=F32
            )
            dx[:, cols] += one + two

    @pl.loop(0, s // tile)
    def _(j):
        cols = pl.ds(pl.multiple_of(j * tile, 128), tile)
        lined = jnp.dot(perm[1], dx[:, cols].astype(BF16), preferred_element_type=F32)
        dxp[:, :, :, cols] = lined.astype(BF16).reshape(2, nz, rows, tile)

    pair = remote(dxp.at[1 - core], pair_in, p_s, p_r, (d, sib))
    pair.start()
    for copy in peak_dp:
        copy.wait()
    peak = stats[...]
    for k in range(1, nd):
        peak = jnp.maximum(peak, st_dp[k - 1])
    stats[...] = peak
    peak_pair = remote(stats, st_pair, sp_s, sp_r, (d, sib))
    peak_pair.start()
    pair.wait_recv()
    line = []
    for k in range(1, nz):
        mixed = dxp[core, z_to[k]].astype(F32) + pair_in[z_to[k]].astype(F32)
        line_out[k - 1] = mixed.astype(BF16)
        copy = remote(line_out.at[k - 1], line_in.at[k - 1], l_s.at[k], l_r.at[k], (d, 2 * z_to[k] + core))
        copy.start()
        line.append(copy)
    peak_pair.wait()
    stats[...] = jnp.maximum(stats[...], st_pair[...])
    peak_line = [
        remote(stats, st_line.at[k - 1], sl_s.at[k], sl_r.at[k], (d, 2 * z_to[k] + core))
        for k in range(1, nz)
    ]
    for copy in peak_line:
        copy.start()
    reduced = dxp[core, z].astype(F32) + pair_in[z].astype(F32)
    for copy in line:
        copy.wait_recv()
    for k in range(1, nz):
        reduced = reduced + line_in[k - 1].astype(F32)
    wide[...] = reduced
    for i in range(nd):
        back[i] = wide[i * tl : (i + 1) * tl, :].astype(BF16)
    home = [
        remote(back.at[dp_to[k]], gtok.at[:, feature_cols(d)], o_s.at[k], o_r.at[k], (dp_to[k], t))
        for k in range(1, nd)
    ]
    for copy in home:
        copy.start()
    gtok[:, feature_cols(d)] = back[d]
    for copy in peak_line:
        copy.wait()
    peak = stats[...]
    for k in range(1, nz):
        peak = jnp.maximum(peak, st_line[k - 1])
    peaks[...] = peak
    for copy in sends + line + [pair]:
        copy.wait_send()

    @pl.loop(0, CHUNKS)
    def _(c):
        for k in range(1, nd):
            partial_copy(c, k).wait_send()
            grad_copy(c, k).wait_send()

    for copy in home:
        copy.wait()


def weight_grads(x, g, gate_out, up_out):
    chunks, nd, _, r, uc = g.shape
    contract = (((0,), (0,)), ((), ()))
    for side, out in ((0, gate_out), (1, up_out)):
        for c in range(chunks):
            out[:, c * uc : (c + 1) * uc] = lax.dot_general(
                x[...], g[c, :, side].reshape(nd * r, uc), contract, preferred_element_type=F32
            ).astype(BF16)


def local(nd, nt, tokens, gate_weight, up_weight, cotangent):
    tl, _ = tokens.shape
    s, units = gate_weight.shape
    r = cotangent.shape[0]
    total = nd * r
    rows = nd * tl
    nz = nt // 2
    uc = units // CHUNKS
    dma = pltpu.SemaphoreType.DMA
    vmem = pl.BlockSpec(memory_space=pltpu.VMEM)
    hbm = pl.BlockSpec(memory_space=pl.ANY)
    weight_bytes = 2 * s * units * 2
    hidden, x, g, grad_tokens, peaks = pl.pallas_call(
        functools.partial(exchange, nd, nt),
        out_shape=(
            jax.ShapeDtypeStruct((r, units), BF16),
            jax.ShapeDtypeStruct((total, s), BF16),
            jax.ShapeDtypeStruct((CHUNKS, nd, 2, r, uc), BF16),
            jax.ShapeDtypeStruct((tl, nd * s), BF16),
            jax.ShapeDtypeStruct((2, 8, 128), F32),
        ),
        in_specs=[vmem, hbm, hbm, vmem],
        out_specs=(vmem,) * 5,
        scratch_shapes=[
            pltpu.VMEM((2, total, total), BF16),
            pltpu.VMEM((s, units), BF16),
            pltpu.VMEM((s, units), BF16),
            pltpu.VMEM((nd, tl, s), BF16),
            pltpu.VMEM((rows, s), F32),
            pltpu.VMEM((nt, rows, s), BF16),
            pltpu.VMEM((CHUNKS, nd, 2, r, uc), BF16),
            pltpu.VMEM((CHUNKS, nd - 1, 2, r, uc), BF16),
            pltpu.VMEM((total, s), F32),
            pltpu.VMEM((2, nz, rows, s), BF16),
            pltpu.VMEM((nz, rows, s), BF16),
            pltpu.VMEM((nz - 1, rows, s), BF16),
            pltpu.VMEM((nz - 1, rows, s), BF16),
            pltpu.VMEM((nd, tl, s), BF16),
            pltpu.VMEM((2, 8, 128), F32),
            pltpu.VMEM((nd - 1, 2, 8, 128), F32),
            pltpu.VMEM((2, 8, 128), F32),
            pltpu.VMEM((nz - 1, 2, 8, 128), F32),
            dma((2, CHUNKS)),
            dma((nd,)), dma((nd,)),
            dma((nz,)), dma((nz,)),
            dma((nz,)), dma((nz,)),
            dma, dma,
            dma((CHUNKS, nd)), dma((CHUNKS, nd)),
            dma((CHUNKS, nd)), dma((CHUNKS, nd)),
            dma((nz,)), dma((nz,)),
            dma((nd,)), dma((nd,)),
            dma((nd,)), dma((nd,)),
            dma, dma,
            dma((nz,)), dma((nz,)),
        ],
        compiler_params=pltpu.CompilerParams(
            collective_id=0, has_side_effects=True, vmem_limit_bytes=48 * 2**20
        ),
        cost_estimate=pl.CostEstimate(
            flops=8 * total * s * units, bytes_accessed=weight_bytes, transcendentals=r * units
        ),
    )(tokens, gate_weight, up_weight, cotangent)

    tile = min(512, s)
    grad_gate, grad_up = pl.pallas_call(
        weight_grads,
        grid=(s // tile,),
        out_shape=(jax.ShapeDtypeStruct((s, units), BF16),) * 2,
        in_specs=[
            pl.BlockSpec((total, tile), lambda i: (0, i)),
            pl.BlockSpec((CHUNKS, nd, 2, r, uc), lambda i: (0, 0, 0, 0, 0)),
        ],
        out_specs=(pl.BlockSpec((tile, units), lambda i: (i, 0)),) * 2,
        compiler_params=pltpu.CompilerParams(vmem_limit_bytes=32 * 2**20),
        cost_estimate=pl.CostEstimate(
            flops=4 * total * s * units, bytes_accessed=weight_bytes, transcendentals=0
        ),
    )(x, g)
    descales = (jnp.max(peaks, axis=(1, 2)) + EPSILON) / FP_MAX
    return (hidden, grad_tokens, grad_gate, grad_up, descales[0], descales[1])


def solution(mesh):
    nd = mesh.shape["dp"]
    nt = mesh.shape["tensor"]
    return jax.shard_map(
        functools.partial(local, nd, nt),
        mesh=mesh,
        in_specs=(
            P(("dp", "tensor"), None),
            P("dp", "tensor"),
            P("dp", "tensor"),
            P("dp", "tensor"),
        ),
        out_specs=(
            P("dp", "tensor"),
            P(("dp", "tensor"), None),
            P("dp", "tensor"),
            P("dp", "tensor"),
            P(),
            P(),
        ),
        check_vma=False,
    )
```

```python
import functools

import jax
import jax.numpy as jnp
from jax import lax
from jax.experimental import pallas as pl
from jax.experimental.pallas import tpu as pltpu
from jax.sharding import PartitionSpec as P

FP_MAX = 448.0
EPSILON = 1e-06
CHUNKS = 4
MESH = pl.DeviceIdType.MESH
F32 = jnp.float32
BF16 = jnp.bfloat16


def remote(src, dst, send, recv, device):
    return pltpu.make_async_remote_copy(
        src_ref=src, dst_ref=dst, send_sem=send, recv_sem=recv, device_id=device, device_id_type=MESH
    )


def lane_peak(values, rows):
    peak = None
    for at in range(0, values.shape[0], rows):
        for lane in range(0, values.shape[1], 128):
            piece = values[at : at + rows, lane : lane + 128]
            peak = piece if peak is None else jnp.maximum(peak, piece)
    return peak


def exchange(
    nd, nt,
    tok, gate_hbm, up_hbm, cot,
    hid, x, g, gtok, peaks,
    perm, wg, wu, blocks, wide, xt, part, inbox, dx, dxp, pair_in, line_out, line_in, back,
    stats, st_dp, st_pair, st_line,
    w_sem, a_s, a_r, b_s, b_r, f_s, f_r, p_s, p_r, rs_s, rs_r, ag_s, ag_r,
    l_s, l_r, o_s, o_r, sd_s, sd_r, sp_s, sp_r, sl_s, sl_r,
):
    d = lax.axis_index("dp")
    t = lax.axis_index("tensor")
    core = lax.rem(t, 2)
    z = t // 2
    nz = nt // 2
    sib = t + 1 - 2 * core
    tl = tok.shape[0]
    s, units = gate_hbm.shape
    r = cot.shape[0]
    total = nd * r
    rows = nd * tl
    uc = units // CHUNKS
    tile = min(512, s)
    dp_to = [lax.rem(d + k, nd) for k in range(nd)]
    z_to = [lax.rem(z + k, nz) for k in range(nz)]
    z_from = [lax.rem(z + nz - k, nz) for k in range(nz)]

    def weight_copies(c):
        cols = pl.ds(pl.multiple_of(c * uc, 128), uc)
        return (
            pltpu.make_async_copy(gate_hbm.at[:, cols], wg.at[:, cols], w_sem.at[0, c]),
            pltpu.make_async_copy(up_hbm.at[:, cols], wu.at[:, cols], w_sem.at[1, c]),
        )

    barrier = pltpu.get_barrier_semaphore()
    for k in range(1, nd):
        pl.semaphore_signal(barrier, inc=1, device_id=(dp_to[k], t), device_id_type=MESH)
    for k in range(1, nz):
        pl.semaphore_signal(barrier, inc=1, device_id=(d, 2 * z_to[k] + core), device_id_type=MESH)
    pl.semaphore_signal(barrier, inc=1, device_id=(d, sib), device_id_type=MESH)
    pl.semaphore_wait(barrier, nd + nz - 1)

    def feature_cols(i):
        return pl.ds(pl.multiple_of(i * s, 128), s)

    sends = []
    first = []
    for k in range(1, nd):
        copy = remote(tok.at[:, feature_cols(dp_to[k])], blocks.at[d], a_s.at[k], a_r.at[k], (dp_to[k], t))
        copy.start()
        first.append(copy)
    for c in range(CHUNKS):
        for copy in weight_copies(c):
            copy.start()

    blocks[d] = tok[:, feature_cols(d)]
    token_peak = lane_peak(jnp.abs(tok[...].astype(F32)), tl)
    stats[0] = jnp.broadcast_to(jnp.max(token_peak, axis=0, keepdims=True), (8, 128))
    for copy in first:
        copy.wait_recv()
    sends += first
    for i in range(nd):
        wide[i * tl : (i + 1) * tl, :] = blocks[i].astype(F32)
    xt[t] = wide[...].astype(BF16)

    along = [
        remote(xt.at[t], xt.at[t], b_s.at[k], b_r.at[k], (d, 2 * z_to[k] + core)) for k in range(1, nz)
    ]
    for copy in along:
        copy.start()
    across = [remote(xt.at[t], xt.at[t], f_s.at[0], f_r.at[0], (d, sib))]
    across[0].start()
    row = lax.broadcasted_iota(jnp.int32, (total, 1), 0)
    col = lax.broadcasted_iota(jnp.int32, (total, total), 1)
    inner = lax.rem(row, tl)
    arrived = lax.rem(lax.div(row, tl), nt) * rows + lax.div(row, r) * tl + inner
    end = lax.div(row, rows)
    tensor_at = 2 * lax.rem(end, nz) + lax.div(end, nz)
    leaving = lax.rem(lax.div(row, tl), nd) * r + tensor_at * tl + inner
    for i, order in enumerate((arrived, leaving)):
        perm[i] = jnp.where(col == order, 1.0, 0.0).astype(BF16)
    for k in range(1, nz):
        along[k - 1].wait_recv()
        slot = 2 * z_from[k] + core
        copy = remote(xt.at[slot], xt.at[slot], f_s.at[k], f_r.at[k], (d, sib))
        copy.start()
        across.append(copy)
    for copy in across:
        copy.wait_recv()
    sends += along + across

    @pl.loop(0, s // tile)
    def _(j):
        cols = pl.ds(pl.multiple_of(j * tile, 128), tile)
        lined = xt[:, :, cols].reshape(total, tile)
        x[:, cols] = jnp.dot(perm[0], lined, preferred_element_type=F32).astype(BF16)
        dx[:, cols] = jnp.zeros((total, tile), F32)

    def partial_copy(c, k):
        return remote(part.at[c, dp_to[k]], inbox.at[c, k - 1], rs_s.at[c, k], rs_r.at[c, k], (dp_to[k], t))

    wide_tile = min(256, uc)

    @pl.loop(0, CHUNKS)
    def _(c):
        for copy in weight_copies(c):
            copy.wait()
        for side, w in ((0, wg), (1, wu)):
            for at in range(0, uc, wide_tile):
                cols = pl.ds(pl.multiple_of(c * uc + at, 128), wide_tile)
                product = jnp.dot(x[...], w[:, cols], preferred_element_type=F32)
                part[c, :, side, :, at : at + wide_tile] = product.astype(BF16).reshape(nd, r, wide_tile)
        for k in range(1, nd):
            partial_copy(c, k).start()

    def grad_copy(c, k):
        return remote(g.at[c, d], g.at[c, d], ag_s.at[c, k], ag_r.at[c, k], (dp_to[k], t))

    def activate(c, peak):
        for k in range(1, nd):
            partial_copy(c, k).wait_recv()
        cols = pl.ds(pl.multiple_of(c * uc, 128), uc)
        gate = part[c, d, 0].astype(F32)
        up = part[c, d, 1].astype(F32)
        for k in range(1, nd):
            gate = gate + inbox[c, k - 1, 0].astype(F32)
            up = up + inbox[c, k - 1, 1].astype(F32)
        sig = jax.nn.sigmoid(gate)
        silu = gate * sig
        hid[:, cols] = (silu * up).astype(BF16)
        cotangent = cot[:, cols].astype(F32)
        d_gate = cotangent * up * sig * (1.0 + gate * (1.0 - sig))
        d_up = cotangent * silu
        g[c, d, 0] = d_gate.astype(BF16)
        g[c, d, 1] = d_up.astype(BF16)
        for k in range(1, nd):
            grad_copy(c, k).start()
        return jnp.maximum(peak, lane_peak(jnp.maximum(jnp.abs(d_gate), jnp.abs(d_up)), 8))

    stats[1] = lax.fori_loop(0, CHUNKS, activate, jnp.zeros((8, 128), F32))
    peak_dp = [remote(stats, st_dp.at[k - 1], sd_s.at[k], sd_r.at[k], (dp_to[k], t)) for k in range(1, nd)]
    for copy in peak_dp:
        copy.start()

    contract = (((1,), (1,)), ((), ()))

    @pl.loop(0, CHUNKS)
    def _(c):
        for k in range(1, nd):
            grad_copy(c, k).wait_recv()
        units_here = pl.ds(pl.multiple_of(c * uc, 128), uc)

        @pl.loop(0, s // tile)
        def _(j):
            cols = pl.ds(pl.multiple_of(j * tile, 128), tile)
            one = lax.dot_general(
                g[c, :, 0].reshape(total, uc), wg[cols, units_here], contract, preferred_element_type=F32
            )
            two = lax.dot_general(
                g[c, :, 1].reshape(total, uc), wu[cols, units_here], contract, preferred_element_type=F32
            )
            dx[:, cols] += one + two

    @pl.loop(0, s // tile)
    def _(j):
        cols = pl.ds(pl.multiple_of(j * tile, 128), tile)
        lined = jnp.dot(perm[1], dx[:, cols].astype(BF16), preferred_element_type=F32)
        dxp[:, :, :, cols] = lined.astype(BF16).reshape(2, nz, rows, tile)

    pair = remote(dxp.at[1 - core], pair_in, p_s, p_r, (d, sib))
    pair.start()
    for copy in peak_dp:
        copy.wait()
    peak = stats[...]
    for k in range(1, nd):
        peak = jnp.maximum(peak, st_dp[k - 1])
    stats[...] = peak
    peak_pair = remote(stats, st_pair, sp_s, sp_r, (d, sib))
    peak_pair.start()
    pair.wait_recv()
    line = []
    for k in range(1, nz):
        mixed = dxp[core, z_to[k]].astype(F32) + pair_in[z_to[k]].astype(F32)
        line_out[k - 1] = mixed.astype(BF16)
        copy = remote(line_out.at[k - 1], line_in.at[k - 1], l_s.at[k], l_r.at[k], (d, 2 * z_to[k] + core))
        copy.start()
        line.append(copy)
    peak_pair.wait()
    stats[...] = jnp.maximum(stats[...], st_pair[...])
    peak_line = [
        remote(stats, st_line.at[k - 1], sl_s.at[k], sl_r.at[k], (d, 2 * z_to[k] + core))
        for k in range(1, nz)
    ]
    for copy in peak_line:
        copy.start()
    reduced = dxp[core, z].astype(F32) + pair_in[z].astype(F32)
    for copy in line:
        copy.wait_recv()
    for k in range(1, nz):
        reduced = reduced + line_in[k - 1].astype(F32)
    wide[...] = reduced
    for i in range(nd):
        back[i] = wide[i * tl : (i + 1) * tl, :].astype(BF16)
    home = [
        remote(back.at[dp_to[k]], gtok.at[:, feature_cols(d)], o_s.at[k], o_r.at[k], (dp_to[k], t))
        for k in range(1, nd)
    ]
    for copy in home:
        copy.start()
    gtok[:, feature_cols(d)] = back[d]
    for copy in peak_line:
        copy.wait()
    peak = stats[...]
    for k in range(1, nz):
        peak = jnp.maximum(peak, st_line[k - 1])
    peaks[...] = peak
    for copy in sends + line + [pair]:
        copy.wait_send()

    @pl.loop(0, CHUNKS)
    def _(c):
        for k in range(1, nd):
            partial_copy(c, k).wait_send()
            grad_copy(c, k).wait_send()

    for copy in home:
        copy.wait()


def weight_grads(x, g, gate_out, up_out):
    chunks, nd, _, r, uc = g.shape
    contract = (((0,), (0,)), ((), ()))
    for side, out in ((0, gate_out), (1, up_out)):
        for c in range(chunks):
            out[:, c * uc : (c + 1) * uc] = lax.dot_general(
                x[...], g[c, :, side].reshape(nd * r, uc), contract, preferred_element_type=F32
            ).astype(BF16)


def local(nd, nt, tokens, gate_weight, up_weight, cotangent):
    tl, _ = tokens.shape
    s, units = gate_weight.shape
    r = cotangent.shape[0]
    total = nd * r
    rows = nd * tl
    nz = nt // 2
    uc = units // CHUNKS
    dma = pltpu.SemaphoreType.DMA
    vmem = pl.BlockSpec(memory_space=pltpu.VMEM)
    hbm = pl.BlockSpec(memory_space=pl.ANY)
    weight_bytes = 2 * s * units * 2
    hidden, x, g, grad_tokens, peaks = pl.pallas_call(
        functools.partial(exchange, nd, nt),
        out_shape=(
            jax.ShapeDtypeStruct((r, units), BF16),
            jax.ShapeDtypeStruct((total, s), BF16),
            jax.ShapeDtypeStruct((CHUNKS, nd, 2, r, uc), BF16),
            jax.ShapeDtypeStruct((tl, nd * s), BF16),
            jax.ShapeDtypeStruct((2, 8, 128), F32),
        ),
        in_specs=[vmem, hbm, hbm, vmem],
        out_specs=(vmem,) * 5,
        scratch_shapes=[
            pltpu.VMEM((2, total, total), BF16),
            pltpu.VMEM((s, units), BF16),
            pltpu.VMEM((s, units), BF16),
            pltpu.VMEM((nd, tl, s), BF16),
            pltpu.VMEM((rows, s), F32),
            pltpu.VMEM((nt, rows, s), BF16),
            pltpu.VMEM((CHUNKS, nd, 2, r, uc), BF16),
            pltpu.VMEM((CHUNKS, nd - 1, 2, r, uc), BF16),
            pltpu.VMEM((total, s), F32),
            pltpu.VMEM((2, nz, rows, s), BF16),
            pltpu.VMEM((nz, rows, s), BF16),
            pltpu.VMEM((nz - 1, rows, s), BF16),
            pltpu.VMEM((nz - 1, rows, s), BF16),
            pltpu.VMEM((nd, tl, s), BF16),
            pltpu.VMEM((2, 8, 128), F32),
            pltpu.VMEM((nd - 1, 2, 8, 128), F32),
            pltpu.VMEM((2, 8, 128), F32),
            pltpu.VMEM((nz - 1, 2, 8, 128), F32),
            dma((2, CHUNKS)),
            dma((nd,)), dma((nd,)),
            dma((nz,)), dma((nz,)),
            dma((nz,)), dma((nz,)),
            dma, dma,
            dma((CHUNKS, nd)), dma((CHUNKS, nd)),
            dma((CHUNKS, nd)), dma((CHUNKS, nd)),
            dma((nz,)), dma((nz,)),
            dma((nd,)), dma((nd,)),
            dma((nd,)), dma((nd,)),
            dma, dma,
            dma((nz,)), dma((nz,)),
        ],
        compiler_params=pltpu.CompilerParams(
            collective_id=0, has_side_effects=True, vmem_limit_bytes=48 * 2**20
        ),
        cost_estimate=pl.CostEstimate(
            flops=8 * total * s * units, bytes_accessed=weight_bytes, transcendentals=r * units
        ),
    )(tokens, gate_weight, up_weight, cotangent)

    tile = min(512, s)
    grad_gate, grad_up = pl.pallas_call(
        weight_grads,
        grid=(s // tile,),
        out_shape=(jax.ShapeDtypeStruct((s, units), BF16),) * 2,
        in_specs=[
            pl.BlockSpec((total, tile), lambda i: (0, i)),
            pl.BlockSpec((CHUNKS, nd, 2, r, uc), lambda i: (0, 0, 0, 0, 0)),
        ],
        out_specs=(pl.BlockSpec((tile, units), lambda i: (i, 0)),) * 2,
        compiler_params=pltpu.CompilerParams(vmem_limit_bytes=32 * 2**20),
        cost_estimate=pl.CostEstimate(
            flops=4 * total * s * units, bytes_accessed=weight_bytes, transcendentals=0
        ),
    )(x, g)
    descales = (jnp.max(peaks, axis=(1, 2)) + EPSILON) / FP_MAX
    return (hidden, grad_tokens, grad_gate, grad_up, descales[0], descales[1])


def solution(mesh):
    nd = mesh.shape["dp"]
    nt = mesh.shape["tensor"]
    return jax.shard_map(
        functools.partial(local, nd, nt),
        mesh=mesh,
        in_specs=(
            P(("dp", "tensor"), None),
            P("dp", "tensor"),
            P("dp", "tensor"),
            P("dp", "tensor"),
        ),
        out_specs=(
            P("dp", "tensor"),
            P(("dp", "tensor"), None),
            P("dp", "tensor"),
            P("dp", "tensor"),
            P(),
            P(),
        ),
        check_vma=False,
    )
```
